128 devices in a mesh: dp: 16 (over z, y_lo, core), tensor: 8 (over x, y_hi).
Axes of the slice: x: 4, y: 4 (y_hi: 2, y_lo: 2; y = y_hi * 2 + y_lo), z: 4, core: 2. Of those that a mesh axis runs over, the one named last changes fastest.
Arguments:
- activations: bfloat16 [3072, 4096], P('dp'), may hold values from -6 to 6
- cotangents: bfloat16 [4, 3072, 4096], P(None, 'dp'), may hold values from -6 to 6
- gate_weight: bfloat16 [4096, 7168], P('dp', 'tensor'), may hold values from -0.09375 to 0.09375
- up_weight: bfloat16 [4096, 7168], P('dp', 'tensor'), may hold values from -0.09375 to 0.09375
- down_weight: bfloat16 [4096, 7168], P('dp', 'tensor'), may hold values from -0.046875 to 0.046875
Outputs:
- input_grad: float32 [3072, 4096], P('dp', 'tensor')
- gate_grad: float32 [4096, 7168], P('dp', 'tensor')
- up_grad: float32 [4096, 7168], P('dp', 'tensor')
- down_grad: float32 [4096, 7168], P('dp', 'tensor')
The draws below stay inside these ranges and needn't reach their ends.
All inputs are finite; a program needn't handle non-finite values.
Results may differ from the reference program's by a relative error of at most 0.0042.
Values may be sent and summed in bfloat16 or wider, within the bound.
No kernel may reach another device: no remote copies, remote signals or barrier semaphores. Data moves between devices by JAX's collectives and lax.ppermute only.
A program may use at most 192 MiB of HBM per device.

```python
import jax
import jax.numpy as jnp

D = 4096
FF = 14336
FF_WIN = 7168
TOKENS = 3072


def levels(key, extent, cuts, least, largest):
    def one(position, parts):
        heights = jax.random.uniform(jax.random.fold_in(jax.random.fold_in(key, 6), position), (parts,), jnp.float32, least / len(cuts), largest / len(cuts))
        return jnp.repeat(jnp.exp(heights), extent[position] // parts).reshape((-1,) + (1,) * (len(extent) - position - 1))

    factor_of = one(*cuts[0])
    for cut in cuts[1:]:
        factor_of = factor_of * one(*cut)
    return factor_of


def noise(key, extent, scale, bound, pieces=(), held_as=jnp.bfloat16):
    drawn = jax.random.normal(key, extent, jnp.float32) * scale
    if len(pieces) > 0:
        drawn = levels(key, extent, pieces, -0.22, 0.18) * drawn
    return jnp.clip(drawn, min=-bound, max=bound).astype(held_as)


def setup_inputs(seed: int = 0) -> dict:
    seeds = jax.random.split(jax.random.key(seed), 6)
    return {
        "activations": noise(seeds[0], (TOKENS, D), 1.0, 6.0, ((0, 16),)),
        "cotangents": noise(seeds[1], (4, TOKENS, D), 1.0, 6.0, ((1, 16),)),
        "gate_weight": noise(seeds[2], (D, FF_WIN), D ** -0.5, 0.09375, ((0, 16), (1, 8))),
        "up_weight": noise(seeds[3], (D, FF_WIN), D ** -0.5, 0.09375, ((0, 16), (1, 8))),
        "down_weight": noise(seeds[4], (D, FF_WIN), FF ** -0.5, 0.046875, ((0, 16), (1, 8))),
    }


def reference(activations, cotangents, gate_weight, up_weight, down_weight):
    gate_pre = jnp.dot(activations, gate_weight, preferred_element_type=jnp.float32)
    up_pre = jnp.dot(activations, up_weight, preferred_element_type=jnp.float32)
    sigmoid_gate = jax.nn.sigmoid(gate_pre)
    silu_gate = gate_pre * sigmoid_gate
    hidden = (silu_gate * up_pre).astype(jnp.bfloat16)
    bounds = [0, FF // 8, FF // 4, FF // 2, FF]
    grad_parts = []
    down_parts = []
    for level in range(4):
        low_unit = bounds[level]
        high_unit = min(bounds[level + 1], FF_WIN)
        if low_unit < high_unit:
            total = jnp.zeros(activations.shape, jnp.float32)
            for later in range(level, 4):
                total = total + cotangents[later].astype(jnp.float32)
            carried = total.astype(jnp.bfloat16)
            unit_slice = down_weight[:, low_unit:high_unit]
            grad_parts.append(jnp.dot(carried, unit_slice, preferred_element_type=jnp.float32))
            down_parts.append(jnp.dot(carried.T, hidden[:, low_unit:high_unit], preferred_element_type=jnp.float32))
    hidden_grad = jnp.concatenate(grad_parts, axis=1)
    down_grad = jnp.concatenate(down_parts, axis=1)
    up_delta = (hidden_grad * silu_gate).astype(jnp.bfloat16)
    gate_delta = (hidden_grad * up_pre * sigmoid_gate * (1.0 + gate_pre * (1.0 - sigmoid_gate))).astype(jnp.bfloat16)
    input_grad = jnp.dot(gate_delta, gate_weight.T, preferred_element_type=jnp.float32) + jnp.dot(up_delta, up_weight.T, preferred_element_type=jnp.float32)
    gate_grad = jnp.dot(activations.T, gate_delta, preferred_element_type=jnp.float32)
    up_grad = jnp.dot(activations.T, up_delta, preferred_element_type=jnp.float32)
    return input_grad, gate_grad, up_grad, down_grad
```

```python
import jax
import jax.numpy as jnp
from jax import lax
from jax.sharding import PartitionSpec as P

FF = 14336
F32 = jnp.float32
BF16 = jnp.bfloat16


def _split(device):
    dp, tensor = divmod(device, 8)
    return dp // 4, (dp // 2) % 2, dp % 2, tensor // 2, tensor % 2


def _join(z, yl, c, x, yh):
    return ((z % 4) * 4 + yl * 2 + c) * 8 + (x % 4) * 2 + yh


def _move(value, where):
    pairs = [(d, _join(*where(*_split(d)))) for d in range(128)]
    return lax.ppermute(value, ("dp", "tensor"), pairs)


def z_shift(value, by):
    return _move(value, lambda z, yl, c, x, yh: (z + by, yl, c, x, yh))


def x_shift(value, by):
    return _move(value, lambda z, yl, c, x, yh: (z, yl, c, x + by, yh))


def core_swap(value):
    return _move(value, lambda z, yl, c, x, yh: (z, yl, 1 - c, x, yh))


def y_swap(value):
    return _move(value, lambda z, yl, c, x, yh: (z, 1 - yl, c, x, yh))


def y_cross(value):
    return _move(value, lambda z, yl, c, x, yh: (z, 1 - yl, c, x, 1 - yh))


def gather_rows(block):
    after, before = z_shift(block, -1), z_shift(block, 1)
    far = jnp.concatenate([z_shift(after[:128], -1), z_shift(before[128:], 1)], axis=0)
    return [block, after, far, before]


def gather_tokens(mine, z, yl, c):
    blocks = mine.reshape(192, 16, 256).transpose(1, 0, 2)

    def pick(to_yl, to_c):
        return jnp.stack(
            [
                lax.dynamic_index_in_dim(
                    blocks, ((z + k) % 4) * 4 + to_yl * 2 + to_c, 0, keepdims=False
                )
                for k in range(4)
            ]
        )

    kept, far = pick(yl, c), pick(1 - yl, c)
    sibling = core_swap(jnp.stack([pick(yl, 1 - c), pick(1 - yl, 1 - c)]))
    other = y_swap(far)
    other_sibling = y_cross(sibling[1])
    return jnp.concatenate([kept, other, sibling[0], other_sibling], axis=1)


def add_over_rows(tokens, rows, link_type):
    total = sum(
        jnp.dot(tokens[k], rows[k], preferred_element_type=F32) for k in (0, 1, 3)
    ) + jnp.dot(tokens[2], rows[2], preferred_element_type=F32)
    half = total[:384] + core_swap(total[384:])
    return half[:192] + y_swap(half[192:].astype(link_type)).astype(F32)


def gather_units(mine):
    pair = jnp.concatenate([mine, y_swap(mine)], axis=0)
    return jnp.concatenate([pair, core_swap(pair)], axis=0)


def scatter_ring(blocks, shift):
    half = blocks[0].shape[0] // 2
    far = blocks[2].astype(BF16)
    low, high = shift(far[:half], 1), shift(far[half:], -1)
    ahead = jnp.concatenate([blocks[1][:half] + low.astype(F32), blocks[1][half:]], axis=0)
    behind = jnp.concatenate([blocks[3][:half], blocks[3][half:] + high.astype(F32)], axis=0)
    return (
        blocks[0]
        + shift(ahead.astype(BF16), 1).astype(F32)
        + shift(behind.astype(BF16), -1).astype(F32)
    )


def weight_gradient(tokens, units):
    over_tokens = (((0,), (0,)), ((), ()))
    blocks = [
        lax.dot_general(tokens[k], units, over_tokens, preferred_element_type=F32)
        for k in range(4)
    ]
    return scatter_ring(blocks, z_shift)


def local(activations, cotangents, gate_weight, up_weight, down_weight):
    dp, tensor = lax.axis_index("dp"), lax.axis_index("tensor")
    z, yl, c = dp // 4, (dp // 2) % 2, dp % 2
    x, yh = tensor // 2, tensor % 2
    gate_rows = gather_rows(gate_weight)
    up_rows = gather_rows(up_weight)
    down_rows = gather_rows(down_weight)

    unit_count = gate_weight.shape[1]
    first_unit = tensor * unit_count
    band_index = (
        1
        + (first_unit >= FF // 8).astype(jnp.int32)
        + (first_unit >= FF // 4).astype(jnp.int32)
        + (first_unit >= FF // 2).astype(jnp.int32)
    )
    summed = jnp.zeros(activations.shape, F32)
    for later in range(4):
        included = (later + 1 >= band_index).astype(F32)
        summed = summed + included * cotangents[later].astype(F32)
    carried = summed.astype(BF16)

    tokens = gather_tokens(activations, z, yl, c)
    cotangent = gather_tokens(carried, z, yl, c)

    gate_pre = add_over_rows(tokens, gate_rows, F32)
    up_pre = add_over_rows(tokens, up_rows, F32)
    hidden_grad = add_over_rows(cotangent, down_rows, BF16)
    sigmoid_gate = jax.nn.sigmoid(gate_pre)
    silu_gate = gate_pre * sigmoid_gate
    hidden = gather_units((silu_gate * up_pre).astype(BF16))
    down_grad = weight_gradient(cotangent, hidden)
    gate_delta = gather_units(
        (hidden_grad * up_pre * sigmoid_gate * (1.0 + gate_pre * (1.0 - sigmoid_gate))).astype(BF16)
    )
    up_delta = gather_units((hidden_grad * silu_gate).astype(BF16))

    gate_grad = weight_gradient(tokens, gate_delta)
    up_grad = weight_gradient(tokens, up_delta)

    over_units = (((1,), (1,)), ((), ()))
    partial = jnp.stack(
        [
            lax.dot_general(gate_delta, gate_rows[k], over_units, preferred_element_type=F32)
            + lax.dot_general(up_delta, up_rows[k], over_units, preferred_element_type=F32)
            for k in range(4)
        ]
    )
    along_x = [
        lax.dynamic_index_in_dim(partial, (x + j - z) % 4, 0, keepdims=False) for j in range(4)
    ]
    columns = scatter_ring(along_x, x_shift).reshape(2, 2, 192, 256)
    halves = []
    for j in range(2):
        moved = []
        for i in range(2):
            block = lax.dynamic_index_in_dim(columns[j], (i + yh + yl) % 2, 0, keepdims=False)
            moved.append(
                _move(
                    block,
                    lambda z, yl, c, x, yh, i=i, j=j: (z, yh ^ i, c ^ j, x, yl),
                )
            )
        halves.append(moved[0] + moved[1])
    input_grad = jnp.where(
        c == 0,
        jnp.concatenate([halves[0], halves[1]], axis=1),
        jnp.concatenate([halves[1], halves[0]], axis=1),
    )
    return (input_grad, gate_grad, up_grad, down_grad)


def solution(mesh):
    return jax.shard_map(
        local,
        mesh=mesh,
        in_specs=(
            P("dp", None),
            P(None, "dp", None),
            P("dp", "tensor"),
            P("dp", "tensor"),
            P("dp", "tensor"),
        ),
        out_specs=(P("dp", "tensor"), P("dp", "tensor"), P("dp", "tensor"), P("dp", "tensor")),
        check_vma=False,
    )
```

```python
import functools

import jax
import jax.numpy as jnp
from jax import lax
from jax.experimental import pallas as pl
from jax.experimental.pallas import tpu as pltpu
from jax.sharding import PartitionSpec as P

FF = 14336
F32 = jnp.float32
BF16 = jnp.bfloat16
VMEM = pl.BlockSpec(memory_space=pltpu.VMEM)
SMEM = pl.BlockSpec(memory_space=pltpu.SMEM)
PARAMS = pltpu.CompilerParams(vmem_limit_bytes=32 * 1024 * 1024)


def _split(device):
    dp, tensor = divmod(device, 8)
    return dp // 4, (dp // 2) % 2, dp % 2, tensor // 2, tensor % 2


def _join(z, yl, c, x, yh):
    return ((z % 4) * 4 + yl * 2 + c) * 8 + (x % 4) * 2 + yh


def _move(value, where):
    pairs = [(d, _join(*where(*_split(d)))) for d in range(128)]
    return lax.ppermute(value, ("dp", "tensor"), pairs)


def z_shift(value, by):
    return _move(value, lambda z, yl, c, x, yh: (z + by, yl, c, x, yh))


def x_shift(value, by):
    return _move(value, lambda z, yl, c, x, yh: (z, yl, c, x + by, yh))


def core_swap(value):
    return _move(value, lambda z, yl, c, x, yh: (z, yl, 1 - c, x, yh))


def y_swap(value):
    return _move(value, lambda z, yl, c, x, yh: (z, 1 - yl, c, x, yh))


def y_cross(value):
    return _move(value, lambda z, yl, c, x, yh: (z, 1 - yl, c, x, 1 - yh))


def after(value, *others):
    return lax.optimization_barrier((value, *others))[0]


def cost(flops, bytes_accessed):
    return pl.CostEstimate(flops=flops, bytes_accessed=bytes_accessed, transcendentals=0)


def _columns(source, block):
    return pl.ds(pl.multiple_of(source[block] * 256, 256), 256)


def _place(block, kept, far, sibling, sibling_far, value):
    (kept, far, sibling, sibling_far)[block // 4][block % 4] = value


def arrange_kernel(source, x, *outs):
    for block in range(16):
        _place(block, *outs, x[:, _columns(source, block)])


def carry_kernel(source, included, x, *outs):
    for block in range(16):
        columns = _columns(source, block)
        total = jnp.zeros((x.shape[1], 256), F32)
        for later in range(4):
            total = total + included[later].astype(F32) * x[later, :, columns].astype(F32)
        _place(block, *outs, total.astype(BF16))


def arrange(kernel, scalars, array):
    rows = 48
    block = (rows, 4096) if array.ndim == 2 else (4, rows, 4096)
    index = (lambda i, *_: (i, 0)) if array.ndim == 2 else (lambda i, *_: (0, i, 0))
    return pl.pallas_call(
        kernel,
        grid_spec=pltpu.PrefetchScalarGridSpec(
            num_scalar_prefetch=len(scalars),
            grid=(192 // rows,),
            in_specs=[pl.BlockSpec(block, index)],
            out_specs=[pl.BlockSpec((4, rows, 256), lambda i, *_: (0, i, 0))] * 4,
        ),
        out_shape=[jax.ShapeDtypeStruct((4, 192, 256), BF16)] * 4,
        compiler_params=PARAMS,
        cost_estimate=cost(0, array.size * 2 + 192 * 4096 * 2),
    )(*scalars, array)


def spread(kept, far, sibling, sibling_far):
    other = y_swap(far)
    from_sibling, from_sibling_far = core_swap(sibling), core_swap(sibling_far)
    return (kept, other, from_sibling, y_cross(from_sibling_far))


def turned(pieces):
    return jnp.concatenate(pieces, axis=1).transpose(0, 2, 1).reshape(1024, 768)


def pre_kernel(t0, t1, t2, t3, w0, w1, w2a, w2b, w3, keep, send, left, right):
    right[0:256] = w0[...]
    right[256:512] = w1[...]
    right[512:640] = w2a[...]
    right[640:768] = w2b[...]
    right[768:1024] = w3[...]
    for out, first, second in ((send, t2, t3), (keep, t0, t1)):
        for k in range(4):
            left[0:192, k * 256 : (k + 1) * 256] = first[k]
            left[192:384, k * 256 : (k + 1) * 256] = second[k]
        out[...] = jnp.dot(left[...], right[...], preferred_element_type=F32)


def partial_pre(pieces, rows):
    return pl.pallas_call(
        pre_kernel,
        in_specs=[VMEM] * 9,
        out_specs=[VMEM] * 2,
        out_shape=[jax.ShapeDtypeStruct((384, 896), F32)] * 2,
        scratch_shapes=[pltpu.VMEM((384, 1024), BF16), pltpu.VMEM((1024, 896), BF16)],
        compiler_params=PARAMS,
        cost_estimate=cost(2 * 768 * 1024 * 896, 6_000_000),
    )(*pieces, *rows)


def gather_rows(block, behind=None):
    if behind is not None:
        block = after(block, behind)
    nxt, prev = z_shift(block, -1), z_shift(block, 1)
    return (block, nxt, z_shift(nxt[:128], -1), z_shift(prev[128:], 1), prev)


def add_over_rows(pieces, rows):
    keep, send = partial_pre(pieces, rows)
    half = keep + core_swap(send)
    other = y_swap(half.astype(BF16)).astype(F32)
    return half + jnp.concatenate([other[192:], other[:192]], axis=0)


def grad_kernel(tokens, mine, theirs, g0, g1, g2a, g2b, g3, right):
    right[0:384] = mine[...]
    right[384:768] = theirs[...]
    for k in range(4):
        block = jnp.dot(
            tokens[k * 256 : (k + 1) * 256, :], right[...], preferred_element_type=F32
        )
        if k == 2:
            g2a[...] = block[:128].astype(BF16)
            g2b[...] = block[128:].astype(BF16)
        else:
            (g0, g1, None, g3)[k][...] = block


def weight_gradient(tokens, units):
    full = jax.ShapeDtypeStruct((256, 896), F32)
    half = jax.ShapeDtypeStruct((128, 896), BF16)
    blocks = pl.pallas_call(
        grad_kernel,
        in_specs=[VMEM] * 3,
        out_specs=[VMEM] * 5,
        out_shape=[full, full, half, half, full],
        scratch_shapes=[pltpu.VMEM((768, 896), BF16)],
        compiler_params=PARAMS,
        cost_estimate=cost(2 * 768 * 1024 * 896, 6_000_000),
    )(tokens, *units)
    return scatter_ring(blocks, z_shift)


def input_kernel(order, *refs):
    gm, gs, um, us = refs[:4]
    gate_rows, up_rows = refs[4:9], refs[9:14]
    j0, j1, j2a, j2b, j3, gate, up = refs[14:]
    for rows, whole in ((gate_rows, gate), (up_rows, up)):
        whole[0] = rows[0][...]
        whole[1] = rows[1][...]
        whole[2, 0:128] = rows[2][...]
        whole[2, 128:256] = rows[3][...]
        whole[3] = rows[4][...]
    over_units = (((1,), (1,)), ((), ()))
    for j in range(4):
        k = order[j]
        for part, (gd, ud) in enumerate(((gm, um), (gs, us))):
            block = lax.dot_general(
                gd[...], gate[k], over_units, preferred_element_type=F32
            ) + lax.dot_general(ud[...], up[k], over_units, preferred_element_type=F32)
            if j == 2:
                (j2a, j2b)[part][...] = block.astype(BF16)
            else:
                (j0, j1, None, j3)[j][part * 384 : (part + 1) * 384, :] = block


def input_partial(order, gate_delta, up_delta, gate_rows, up_rows):
    full = jax.ShapeDtypeStruct((768, 256), F32)
    half = jax.ShapeDtypeStruct((384, 256), BF16)
    return pl.pallas_call(
        input_kernel,
        in_specs=[SMEM] + [VMEM] * 14,
        out_specs=[VMEM] * 5,
        out_shape=[full, full, half, half, full],
        scratch_shapes=[pltpu.VMEM((4, 256, 896), BF16)] * 2,
        compiler_params=PARAMS,
        cost_estimate=cost(4 * 768 * 1024 * 896, 10_000_000),
    )(order, *gate_delta, *up_delta, *gate_rows, *up_rows)


def scatter_ring(blocks, shift):
    b0, b1, b2a, b2b, b3 = blocks
    half = b2a.shape[0]
    low, high = shift(b2a, 1), shift(b2b, -1)
    ahead = jnp.concatenate(
        [(b1[:half] + low.astype(F32)).astype(BF16), b1[half:].astype(BF16)], axis=0
    )
    behind = jnp.concatenate(
        [b3[:half].astype(BF16), (b3[half:] + high.astype(F32)).astype(BF16)], axis=0
    )
    return b0 + shift(ahead, 1).astype(F32) + shift(behind, -1).astype(F32)


def local(activations, cotangents, gate_weight, up_weight, down_weight):
    dp, tensor = lax.axis_index("dp"), lax.axis_index("tensor")
    z, yl, c = dp // 4, (dp // 2) % 2, dp % 2
    x, yh = tensor // 2, tensor % 2
    source = jnp.stack(
        [
            ((z + k) % 4) * 4 + (yl ^ far) * 2 + (c ^ sibling)
            for sibling in range(2)
            for far in range(2)
            for k in range(4)
        ]
    ).astype(jnp.int32)
    first_unit = tensor * gate_weight.shape[1]
    band_index = (
        1
        + (first_unit >= FF // 8).astype(jnp.int32)
        + (first_unit >= FF // 4).astype(jnp.int32)
        + (first_unit >= FF // 2).astype(jnp.int32)
    )
    included = jnp.stack([(k + 1 >= band_index).astype(jnp.int32) for k in range(4)])

    gate_rows = gather_rows(gate_weight)
    up_rows = gather_rows(up_weight)
    down_rows = gather_rows(down_weight, gate_rows[1])

    tokens = spread(*arrange(arrange_kernel, (source,), activations))
    cotangent = spread(*arrange(carry_kernel, (source, included), cotangents))
    tokens_turned, cotangent_turned = turned(tokens), turned(cotangent)

    gate_pre = add_over_rows(tokens, gate_rows)
    up_pre = add_over_rows(tokens, up_rows)
    sigmoid_gate = jax.nn.sigmoid(gate_pre)
    silu_gate = gate_pre * sigmoid_gate
    hidden = (silu_gate * up_pre).astype(BF16)
    hidden, gate_pre, up_pre = lax.optimization_barrier((hidden, gate_pre, up_pre))
    down_grad = weight_gradient(cotangent_turned, (hidden, core_swap(hidden)))

    hidden_grad = add_over_rows(cotangent, down_rows)
    sigmoid_gate = jax.nn.sigmoid(gate_pre)
    silu_gate = gate_pre * sigmoid_gate
    gate_mine = (
        hidden_grad * up_pre * sigmoid_gate * (1.0 + gate_pre * (1.0 - sigmoid_gate))
    ).astype(BF16)
    up_mine = (hidden_grad * silu_gate).astype(BF16)
    gate_delta = (gate_mine, core_swap(gate_mine))
    up_delta = (up_mine, core_swap(up_mine))

    gate_grad = weight_gradient(tokens_turned, gate_delta)
    up_grad = weight_gradient(tokens_turned, up_delta)

    order = jnp.stack([(x + j - z) % 4 for j in range(4)]).astype(jnp.int32)
    along_x = input_partial(order, gate_delta, up_delta, gate_rows, up_rows)
    columns = scatter_ring(along_x, x_shift).reshape(2, 2, 192, 256)
    halves = []
    for j in range(2):
        moved = []
        for i in range(2):
            block = lax.dynamic_index_in_dim(columns[j], (i + yh + yl) % 2, 0, keepdims=False)
            moved.append(
                _move(block, lambda z, yl, c, x, yh, i=i, j=j: (z, yh ^ i, c ^ j, x, yl))
            )
        halves.append(moved[0] + moved[1])
    input_grad = jnp.where(
        c == 0,
        jnp.concatenate([halves[0], halves[1]], axis=1),
        jnp.concatenate([halves[1], halves[0]], axis=1),
    )
    return (input_grad, gate_grad, up_grad, down_grad)


def solution(mesh):
    return jax.shard_map(
        local,
        mesh=mesh,
        in_specs=(
            P("dp", None),
            P(None, "dp", None),
            P("dp", "tensor"),
            P("dp", "tensor"),
            P("dp", "tensor"),
        ),
        out_specs=(P("dp", "tensor"), P("dp", "tensor"), P("dp", "tensor"), P("dp", "tensor")),
        check_vma=False,
    )
```

```python
import functools

import jax
import jax.numpy as jnp
from jax import lax
from jax.experimental import pallas as pl
from jax.experimental.pallas import tpu as pltpu
from jax.sharding import PartitionSpec as P

FF = 14336
F32 = jnp.float32
BF16 = jnp.bfloat16
CHUNKS = (384, 512)
SCALE = 1.0
VMEM = pl.BlockSpec(memory_space=pltpu.VMEM)
SMEM = pl.BlockSpec(memory_space=pltpu.SMEM)
PARAMS = pltpu.CompilerParams(vmem_limit_bytes=32 * 1024 * 1024)


def _split(device):
    dp, tensor = divmod(device, 8)
    return dp // 4, (dp // 2) % 2, dp % 2, tensor // 2, tensor % 2


def _join(z, yl, c, x, yh):
    return ((z % 4) * 4 + yl * 2 + c) * 8 + (x % 4) * 2 + yh


def _move(value, where):
    pairs = [(d, _join(*where(*_split(d)))) for d in range(128)]
    return lax.ppermute(value, ("dp", "tensor"), pairs)


def z_shift(value, by):
    return _move(value, lambda z, yl, c, x, yh: (z + by, yl, c, x, yh))


def x_shift(value, by):
    return _move(value, lambda z, yl, c, x, yh: (z, yl, c, x + by, yh))


def core_swap(value):
    return _move(value, lambda z, yl, c, x, yh: (z, yl, 1 - c, x, yh))


def y_swap(value):
    return _move(value, lambda z, yl, c, x, yh: (z, 1 - yl, c, x, yh))


def far_swap(value):
    return _move(value, lambda z, yl, c, x, yh: (z, 1 - yl, 1 - c, x, 1 - yh))


def after(value, *others):
    return lax.optimization_barrier((value, *others))[0]


def shape(*dims, dtype=F32):
    return jax.ShapeDtypeStruct(dims, dtype)


def local_kernel(kernel, outs, microseconds, *args, scalars=0, scratch=()):
    return pl.pallas_call(
        kernel,
        in_specs=[SMEM] * scalars + [VMEM] * (len(args) - scalars),
        out_specs=[VMEM] * len(outs),
        out_shape=outs,
        scratch_shapes=scratch,
        compiler_params=PARAMS,
        cost_estimate=cost(microseconds),
    )(*args)


def cost(microseconds):
    return pl.CostEstimate(
        flops=int(microseconds * SCALE * 1.1e9), bytes_accessed=1000, transcendentals=0
    )


def arrange_kernel(source, included, x, cotangents, *outs):
    for block in range(16):
        columns = pl.ds(pl.multiple_of(source[block] * 256, 256), 256)
        out, k = outs[block // 4], block % 4
        out[0, k] = x[:, columns]
        total = jnp.zeros((x.shape[0], 256), F32)
        for later in range(4):
            total = total + included[later].astype(F32) * cotangents[later, :, columns].astype(F32)
        out[1, k] = total.astype(BF16)


def arrange(source, included, activations, cotangents):
    rows = 48
    return pl.pallas_call(
        arrange_kernel,
        grid_spec=pltpu.PrefetchScalarGridSpec(
            num_scalar_prefetch=2,
            grid=(192 // rows,),
            in_specs=[
                pl.BlockSpec((rows, 4096), lambda i, *_: (i, 0)),
                pl.BlockSpec((4, rows, 4096), lambda i, *_: (0, i, 0)),
            ],
            out_specs=[pl.BlockSpec((2, 4, rows, 256), lambda i, *_: (0, 0, i, 0))] * 4,
        ),
        out_shape=[shape(2, 4, 192, 256, dtype=BF16)] * 4,
        compiler_params=PARAMS,
        cost_estimate=cost(3.0),
    )(source, included, activations, cotangents)


def spread(kept, far, sibling, sibling_far):
    return (kept, y_swap(far), core_swap(sibling), far_swap(sibling_far))


def turn_kernel(t0, t1, t2, t3, *outs):
    for which, out in enumerate(outs):
        for k in range(4):
            whole = jnp.concatenate([t[which, k] for t in (t0, t1, t2, t3)], axis=0)
            out[k * 256 : (k + 1) * 256, :] = whole.T


def fill(rows, far, low, high, own, nxt, prev):
    far[0:384] = low[...]
    far[384:768] = high[...]
    for m in range(rows.shape[0]):
        for k, part in enumerate((own, nxt, far, prev)):
            rows[m, k * 256 : (k + 1) * 256] = part[m * 256 : (m + 1) * 256]


def pre_kernel(t0, t1, t2, t3, own, nxt, low, high, prev, keep, s0, s1, s2, left, rows, far):
    fill(rows, far, low, high, own, nxt, prev)
    for outs, first, second in (((s0, s1, s2), t2, t3), (keep, t0, t1)):
        for which in range(2):
            for k in range(4):
                left[0:192, k * 256 : (k + 1) * 256] = first[which, k]
                left[192:384, k * 256 : (k + 1) * 256] = second[which, k]
            for m in ((0, 1), (2,))[which]:
                block = jnp.dot(left[...], rows[m], preferred_element_type=F32)
                if outs is keep:
                    keep[m] = block
                else:
                    outs[m][...] = block


def delta_kernel(half, other, other_grad, out):
    def part(first, swapped):
        @pl.loop(0, 192 // 16)
        def _(i):
            mine = pl.ds(pl.multiple_of(first + i * 16, 16), 16)
            theirs = pl.ds(pl.multiple_of(swapped + i * 16, 16), 16)
            gate, up = (half[m, mine] + other[m, theirs].astype(F32) for m in range(2))
            grad = half[2, mine] + other_grad[theirs].astype(F32)
            sigmoid = jax.nn.sigmoid(gate)
            silu = gate * sigmoid
            out[0, mine] = (grad * up * sigmoid * (1.0 + gate * (1.0 - sigmoid))).astype(BF16)
            out[1, mine] = (grad * silu).astype(BF16)
            out[2, mine] = (silu * up).astype(BF16)

    part(0, 192)
    part(192, 0)


def grad_kernel(tokens, cotangents, mine, theirs, b0, b1, low, high, b3, right):
    for m in range(3):
        right[0:384] = mine[m]
        right[384:768] = theirs[m]
        left = tokens if m < 2 else cotangents
        for k in (2, 1, 3, 0):
            block = jnp.dot(
                left[k * 256 : (k + 1) * 256, :], right[...], preferred_element_type=F32
            )
            if k != 2:
                (b0, b1, None, b3)[k][m * 256 : (m + 1) * 256] = block
                continue
            block = block.astype(BF16)
            if m == 0:
                low[0:256] = block
            elif m == 1:
                low[256:384] = block[:128]
                high[0:128] = block[128:]
            else:
                high[128:384] = block


def middle_kernel(b1, b3, low, high, ahead, behind):
    ahead[0:384] = (b1[0:384] + low[...].astype(F32)).astype(BF16)
    ahead[384:768] = b1[384:768].astype(BF16)
    behind[0:384] = b3[0:384].astype(BF16)
    behind[384:768] = (b3[384:768] + high[...].astype(F32)).astype(BF16)


def finish_kernel(*refs):
    parts, outs = refs[:-3], refs[-3:]
    for m, out in enumerate(outs):
        rows = slice(m * 256, (m + 1) * 256)
        first = 0
        for i in range(len(parts) // 3):
            b0, r1, r3 = parts[3 * i : 3 * i + 3]
            last = first + b0.shape[1]
            out[:, first:last] = b0[rows] + r1[rows].astype(F32) + r3[rows].astype(F32)
            first = last


def input_kernel(last, has_total, order, mine, theirs, own, nxt, low, high, prev, *refs):
    if has_total:
        total, *refs = refs
    *outs, rows, far = refs
    fill(rows, far, low, high, own, nxt, prev)
    over_units = (((1,), (1,)), ((), ()))
    for j in range(4):
        here = pl.ds(pl.multiple_of(order[j] * 256, 256), 256)
        for part, delta in enumerate((mine, theirs)):
            tokens = slice(part * 384, (part + 1) * 384)
            block = lax.dot_general(
                delta[0], rows[0, here, :], over_units, preferred_element_type=F32
            ) + lax.dot_general(delta[1], rows[1, here, :], over_units, preferred_element_type=F32)
            if has_total:
                block = block + total[j, tokens]
            if last:
                outs[j][tokens] = block.astype(outs[j].dtype)
            else:
                outs[0][j, tokens] = block


def local(activations, cotangents, gate_weight, up_weight, down_weight):
    dp, tensor = lax.axis_index("dp"), lax.axis_index("tensor")
    z, yl, c = dp // 4, (dp // 2) % 2, dp % 2
    x, yh = tensor // 2, tensor % 2
    source = jnp.stack(
        [
            ((z + k) % 4) * 4 + (yl ^ far) * 2 + (c ^ sibling)
            for sibling in range(2)
            for far in range(2)
            for k in range(4)
        ]
    ).astype(jnp.int32)
    first_unit = tensor * gate_weight.shape[1]
    band_index = (
        1
        + (first_unit >= FF // 8).astype(jnp.int32)
        + (first_unit >= FF // 4).astype(jnp.int32)
        + (first_unit >= FF // 2).astype(jnp.int32)
    )
    included = jnp.stack([(k + 1 >= band_index).astype(jnp.int32) for k in range(4)])
    order = jnp.stack([(x + j - z) % 4 for j in range(4)]).astype(jnp.int32)

    rows, first = [], 0
    for width in CHUNKS:
        own = jnp.concatenate(
            [w[:, first : first + width] for w in (gate_weight, up_weight, down_weight)], axis=0
        )
        if rows:
            own = after(own, rows[-1][1])
        nxt, prev = z_shift(own, -1), z_shift(own, 1)
        rows.append((own, nxt, z_shift(nxt[:384], -1), z_shift(prev[384:], 1), prev))
        first += width

    pieces = spread(*arrange(source, included, activations, cotangents))
    turned = local_kernel(turn_kernel, [shape(1024, 768, dtype=BF16)] * 2, 3.0, *pieces)

    halves = []
    for i, width in enumerate(CHUNKS):
        own, nxt, low, high, prev = rows[i]
        late = pieces[0]
        if i == 1:
            late = after(late, halves[0][1], *turned)
        keep, *send = local_kernel(
            pre_kernel,
            [shape(3, 384, width)] + [shape(384, width)] * 3,
            width / 128,
            late,
            *pieces[1:],
            own,
            nxt,
            low,
            high,
            prev,
            scratch=(
                pltpu.VMEM((384, 1024), BF16),
                pltpu.VMEM((3, 1024, width), BF16),
                pltpu.VMEM((768, width), BF16),
            ),
        )
        received = [core_swap(part) for part in send]
        if halves:
            received[0] = after(received[0], halves[-1][2])
        half = keep + jnp.stack(received)
        pair, single = half[:2].astype(BF16), half[2].astype(BF16)
        sent = (pair, single)
        halves.append((half, y_swap(pair), y_swap(single)))
        if i == 0:
            own, nxt, low, high, prev = rows[1]
            nxt_late, prev_late = after(nxt, *sent), after(prev, *sent)
            rows[1] = (own, nxt, z_shift(nxt_late[:384], -1), z_shift(prev_late[384:], 1), prev)

    total, ready, finished = None, None, []
    for i, width in enumerate(CHUNKS):
        half, other, other_grad = halves[i]
        if ready is not None:
            other = after(other, *ready)

        (mine,) = local_kernel(
            delta_kernel, [shape(3, 384, width, dtype=BF16)], width / 256, half, other, other_grad
        )
        theirs = core_swap(mine)
        last = i == len(CHUNKS) - 1
        outs = [shape(4, 768, 256)]
        if last:
            outs = [shape(768, 256)] + [shape(768, 256, dtype=BF16)] * 3
        partial = local_kernel(
            functools.partial(input_kernel, last, total is not None),
            outs,
            width / 128,
            order,
            mine,
            theirs,
            *rows[i],
            *(() if total is None else (total,)),
            scalars=1,
            scratch=(pltpu.VMEM((2, 1024, width), BF16), pltpu.VMEM((768, width), BF16)),
        )
        total = partial[0]
        b0, b1, low, high, b3 = local_kernel(
            grad_kernel,
            [shape(768, width)] * 2
            + [shape(384, width, dtype=BF16)] * 2
            + [shape(768, width)],
            width / 128,
            *turned,
            mine,
            theirs,
            scratch=(pltpu.VMEM((768, width), BF16),),
        )
        ahead, behind = local_kernel(
            middle_kernel,
            [shape(768, width, dtype=BF16)] * 2,
            width / 400,
            b1,
            b3,
            z_shift(low, 1),
            z_shift(high, -1),
        )
        finished += [b0, z_shift(ahead, 1), z_shift(behind, -1)]
        ready = (*finished[-2:], total)
    gate_grad, up_grad, down_grad = local_kernel(
        finish_kernel, [shape(256, sum(CHUNKS))] * 3, 2.0, *finished
    )

    columns = (
        partial[0]
        + x_shift(partial[1], 1).astype(F32)
        + x_shift(partial[2], 2).astype(F32)
        + x_shift(partial[3], -1).astype(F32)
    ).reshape(2, 2, 192, 256)
    sides = []
    for j in range(2):
        moved = []
        for i in range(2):
            block = lax.dynamic_index_in_dim(columns[j], (i + yh + yl) % 2, 0, keepdims=False)
            moved.append(
                _move(block, lambda z, yl, c, x, yh, i=i, j=j: (z, yh ^ i, c ^ j, x, yl))
            )
        sides.append(moved[0] + moved[1])
    input_grad = jnp.where(
        c == 0,
        jnp.concatenate([sides[0], sides[1]], axis=1),
        jnp.concatenate([sides[1], sides[0]], axis=1),
    )
    return (input_grad, gate_grad, up_grad, down_grad)


def solution(mesh):
    return jax.shard_map(
        local,
        mesh=mesh,
        in_specs=(
            P("dp", None),
            P(None, "dp", None),
            P("dp", "tensor"),
            P("dp", "tensor"),
            P("dp", "tensor"),
        ),
        out_specs=(P("dp", "tensor"), P("dp", "tensor"), P("dp", "tensor"), P("dp", "tensor")),
        check_vma=False,
    )
```

```python
import functools

import jax
import jax.numpy as jnp
from jax import lax
from jax.experimental import pallas as pl
from jax.experimental.pallas import tpu as pltpu
from jax.sharding import PartitionSpec as P

FF = 14336
F32 = jnp.float32
BF16 = jnp.bfloat16
CHUNKS = (384, 512)
SCALE = 1.0
CSPLIT = (3,)
YSPLIT = (3,)
W_AFTER = True
MERGE = False
BB_AFTER = True
KB_AFTER = 1
HB_AFTER = 2
GA_AFTER = True
INPUT_FIRST = True
VMEM = pl.BlockSpec(memory_space=pltpu.VMEM)
SMEM = pl.BlockSpec(memory_space=pltpu.SMEM)
PARAMS = pltpu.CompilerParams(vmem_limit_bytes=10 * 1024 * 1024)


def _split(device):
    dp, tensor = divmod(device, 8)
    return dp // 4, (dp // 2) % 2, dp % 2, tensor // 2, tensor % 2


def _join(z, yl, c, x, yh):
    return ((z % 4) * 4 + yl * 2 + c) * 8 + (x % 4) * 2 + yh


def _move(value, where):
    pairs = [(d, _join(*where(*_split(d)))) for d in range(128)]
    return lax.ppermute(value, ("dp", "tensor"), pairs)


def z_shift(value, by):
    return _move(value, lambda z, yl, c, x, yh: (z + by, yl, c, x, yh))


def x_shift(value, by):
    return _move(value, lambda z, yl, c, x, yh: (z, yl, c, x + by, yh))


def core_swap(value):
    return _move(value, lambda z, yl, c, x, yh: (z, yl, 1 - c, x, yh))


def y_swap(value):
    return _move(value, lambda z, yl, c, x, yh: (z, 1 - yl, c, x, yh))


def far_swap(value):
    return _move(value, lambda z, yl, c, x, yh: (z, 1 - yl, 1 - c, x, 1 - yh))


def after(value, *others):
    return lax.optimization_barrier((value, *others))[0]


def shape(*dims, dtype=F32):
    return jax.ShapeDtypeStruct(dims, dtype)


def local_kernel(kernel, outs, microseconds, *args, scalars=0, scratch=()):
    return pl.pallas_call(
        kernel,
        in_specs=[SMEM] * scalars + [VMEM] * (len(args) - scalars),
        out_specs=[VMEM] * len(outs),
        out_shape=outs,
        scratch_shapes=scratch,
        compiler_params=PARAMS,
        cost_estimate=cost(microseconds),
    )(*args)


def cost(microseconds):
    return pl.CostEstimate(
        flops=int(microseconds * SCALE * 1.1e9), bytes_accessed=1000, transcendentals=0
    )


def arrange_kernel(numbers, x, cotangents, *outs):
    for block in range(16):
        columns = pl.ds(pl.multiple_of(numbers[block] * 256, 256), 256)
        out, k = outs[block // 4], block % 4
        out[0, k] = x[:, columns]
        total = jnp.zeros((x.shape[0], 256), F32)
        for later in range(4):
            total = total + numbers[16 + later].astype(F32) * cotangents[later, :, columns].astype(F32)
        out[1, k] = total.astype(BF16)


def arrange(numbers, activations, cotangents):
    rows = 48
    return pl.pallas_call(
        arrange_kernel,
        grid_spec=pltpu.PrefetchScalarGridSpec(
            num_scalar_prefetch=1,
            grid=(192 // rows,),
            in_specs=[
                pl.BlockSpec((rows, 4096), lambda i, *_: (i, 0)),
                pl.BlockSpec((4, rows, 4096), lambda i, *_: (0, i, 0)),
            ],
            out_specs=[pl.BlockSpec((2, 4, rows, 256), lambda i, *_: (0, 0, i, 0))] * 4,
        ),
        out_shape=[shape(2, 4, 192, 256, dtype=BF16)] * 4,
        compiler_params=PARAMS,
        cost_estimate=cost(3.0),
    )(numbers, activations, cotangents)


def spread(kept, far, sibling, sibling_far):
    return (kept, y_swap(far), core_swap(sibling), far_swap(sibling_far))


def turn_kernel(t0, t1, t2, t3, *outs):
    for which, out in enumerate(outs):
        for k in range(4):
            whole = jnp.concatenate([t[which, k] for t in (t0, t1, t2, t3)], axis=0)
            out[k * 256 : (k + 1) * 256, :] = whole.T


def stack_kernel(*refs):
    weights, outs = refs[:3], refs[3:]
    first = 0
    for out in outs:
        last = first + out.shape[1]
        for m, weight in enumerate(weights):
            out[m * 256 : (m + 1) * 256] = weight[:, first:last]
        first = last


def fill(first, rows, far, low, high, own, nxt, prev):
    far[0:384] = low[...]
    far[384:768] = high[...]
    width = rows.shape[2]
    for m in range(rows.shape[0]):
        for k, part in enumerate((own, nxt, far, prev)):
            start = 0 if part is far else first
            rows[m, k * 256 : (k + 1) * 256] = part[
                m * 256 : (m + 1) * 256, start : start + width
            ]


def part_of(parts, m):
    for part in parts:
        if m < part.shape[0]:
            return part.at[m]
        m -= part.shape[0]


def pre_kernel(first, t0, t1, t2, t3, own, nxt, low, high, prev, keep, *refs):
    *sends, left, rows, far = refs
    fill(first, rows, far, low, high, own, nxt, prev)
    for outs, upper, lower in ((sends, t2, t3), ((keep,), t0, t1)):
        for which in range(2):
            for k in range(4):
                left[0:192, k * 256 : (k + 1) * 256] = upper[which, k]
                left[192:384, k * 256 : (k + 1) * 256] = lower[which, k]
            for m in ((0, 1), (2,))[which]:
                part_of(outs, m)[...] = jnp.dot(
                    left[...], rows[m], preferred_element_type=F32
                )


def half_kernel(keep, *refs):
    received, outs = refs[: len(CSPLIT)], refs[len(CSPLIT) :]
    for m in range(3):
        part_of(outs, m)[...] = (keep[m] + part_of(received, m)[...]).astype(BF16)


def cut_kernel(first, nxt, prev, low, high):
    columns = slice(first, first + low.shape[1])
    low[...] = nxt[0:384, columns]
    high[...] = prev[384:768, columns]


def column_kernel(numbers, own, r1, r2, r3, *outs):
    for j in range(2):
        for i in range(2):
            block = (i + numbers[24]) % 2
            rows = pl.ds(pl.multiple_of(j * 384 + block * 192, 192), 192)
            outs[2 * j + i][...] = (
                own[rows]
                + r1[rows].astype(F32)
                + r2[rows].astype(F32)
                + r3[rows].astype(F32)
            )


def place_kernel(numbers, a0, a1, b0, b1, out):
    for j, (first, second) in enumerate(((a0, a1), (b0, b1))):
        side = (j + numbers[25]) % 2
        out[:, pl.ds(pl.multiple_of(side * 256, 256), 256)] = first[...] + second[...]


def delta_kernel(keep, *refs):
    *refs, out = refs
    received, others = refs[: len(CSPLIT)], refs[len(CSPLIT) :]

    def part(first, swapped):
        @pl.loop(0, 192 // 16)
        def _(i):
            mine = pl.ds(pl.multiple_of(first + i * 16, 16), 16)
            theirs = pl.ds(pl.multiple_of(swapped + i * 16, 16), 16)
            gate, up, grad = (
                (keep[m, mine] + part_of(received, m)[mine])
                + part_of(others, m)[theirs].astype(F32)
                for m in range(3)
            )
            sigmoid = jax.nn.sigmoid(gate)
            silu = gate * sigmoid
            out[0, mine] = (grad * up * sigmoid * (1.0 + gate * (1.0 - sigmoid))).astype(BF16)
            out[1, mine] = (grad * silu).astype(BF16)
            out[2, mine] = (silu * up).astype(BF16)

    part(0, 192)
    part(192, 0)


def grad_kernel(tokens, cotangents, mine, theirs, b0, b1, low, high, b3, right):
    for m in range(3):
        right[0:384] = mine[m]
        right[384:768] = theirs[m]
        left = tokens if m < 2 else cotangents
        for k in (2, 1, 3, 0):
            block = jnp.dot(
                left[k * 256 : (k + 1) * 256, :], right[...], preferred_element_type=F32
            )
            if k != 2:
                (b0, b1, None, b3)[k][m * 256 : (m + 1) * 256] = block
                continue
            block = block.astype(BF16)
            if m == 0:
                low[0:256] = block
            elif m == 1:
                low[256:384] = block[:128]
                high[0:128] = block[128:]
            else:
                high[128:384] = block


def middle_kernel(b1, b3, low, high, ahead, behind):
    ahead[0:384] = (b1[0:384] + low[...].astype(F32)).astype(BF16)
    ahead[384:768] = b1[384:768].astype(BF16)
    behind[0:384] = b3[0:384].astype(BF16)
    behind[384:768] = (b3[384:768] + high[...].astype(F32)).astype(BF16)


def finish_kernel(*refs):
    parts, outs = refs[:-3], refs[-3:]
    for m, out in enumerate(outs):
        rows = slice(m * 256, (m + 1) * 256)
        first = 0
        for i in range(len(parts) // 3):
            b0, r1, r3 = parts[3 * i : 3 * i + 3]
            last = first + b0.shape[1]
            out[:, first:last] = b0[rows] + r1[rows].astype(F32) + r3[rows].astype(F32)
            first = last


def input_kernel(first, last, has_total, numbers, mine, theirs, own, nxt, low, high, prev, *refs):
    if has_total:
        total, *refs = refs
    *outs, rows, far = refs
    fill(first, rows, far, low, high, own, nxt, prev)
    over_units = (((1,), (1,)), ((), ()))
    for j in range(4):
        here = pl.ds(pl.multiple_of(numbers[20 + j] * 256, 256), 256)
        for part, delta in enumerate((mine, theirs)):
            tokens = slice(part * 384, (part + 1) * 384)
            block = lax.dot_general(
                delta[0], rows[0, here, :], over_units, preferred_element_type=F32
            ) + lax.dot_general(delta[1], rows[1, here, :], over_units, preferred_element_type=F32)
            if has_total:
                block = block + total[j, tokens]
            if last:
                outs[j][tokens] = block.astype(outs[j].dtype)
            else:
                outs[0][j, tokens] = block


def local(activations, cotangents, gate_weight, up_weight, down_weight):
    dp, tensor = lax.axis_index("dp"), lax.axis_index("tensor")
    z, yl, c = dp // 4, (dp // 2) % 2, dp % 2
    x, yh = tensor // 2, tensor % 2
    first_unit = tensor * gate_weight.shape[1]
    band_index = (
        1
        + (first_unit >= FF // 8).astype(jnp.int32)
        + (first_unit >= FF // 4).astype(jnp.int32)
        + (first_unit >= FF // 2).astype(jnp.int32)
    )
    source = [
        ((z + k) % 4) * 4 + (yl ^ far) * 2 + (c ^ sibling)
        for sibling in range(2)
        for far in range(2)
        for k in range(4)
    ]
    included = [(k + 1 >= band_index).astype(jnp.int32) for k in range(4)]
    order = [(x + j - z) % 4 for j in range(4)]
    numbers = jnp.stack(source + included + order + [(yh + yl) % 2, c]).astype(jnp.int32)

    stacks = local_kernel(
        stack_kernel,
        [shape(768, width, dtype=BF16) for width in ((896,) if MERGE else CHUNKS)],
        1.0,
        gate_weight,
        up_weight,
        down_weight,
    )

    def first_step(own):
        return own, z_shift(own, -1), z_shift(own, 1)

    columns = [0] * len(CHUNKS)
    if MERGE:
        columns = [sum(CHUNKS[:i]) for i in range(len(CHUNKS))]

    def second_step(own, nxt, prev, first, width):
        low, high = local_kernel(
            functools.partial(cut_kernel, first),
            [shape(384, width, dtype=BF16)] * 2,
            0.5,
            nxt,
            prev,
        )
        return own, nxt, z_shift(low, -1), z_shift(high, 1), prev

    pieces = spread(*arrange(numbers, activations, cotangents))
    turned = local_kernel(turn_kernel, [shape(1024, 768, dtype=BF16)] * 2, 1.0, *pieces)

    rows, halves = [], []
    near = first_step(stacks[0])
    for i, width in enumerate(CHUNKS):
        own, nxt, prev = near
        if i and BB_AFTER:
            nxt = after(nxt, *halves[-1][2])
        column = columns[i]
        rows.append(second_step(own, nxt, prev, column, width))
        if i + 1 < len(CHUNKS) and not MERGE:
            near = first_step(after(stacks[i + 1], near[1]) if W_AFTER else stacks[i + 1])
        late = pieces[0]
        if i:
            late = after(late, *turned, *halves[-1][3][:KB_AFTER])
        keep, *send = local_kernel(
            functools.partial(pre_kernel, column),
            [shape(3, 384, width)] + [shape(count, 384, width) for count in CSPLIT],
            2.6,
            late,
            *pieces[1:],
            *rows[i],
            scratch=(
                pltpu.VMEM((384, 1024), BF16),
                pltpu.VMEM((3, 1024, width), BF16),
                pltpu.VMEM((768, width), BF16),
            ),
        )
        received = [core_swap(part) for part in send]
        if i and HB_AFTER:
            received[0] = after(received[0], *halves[-1][3][:HB_AFTER])
        sent = local_kernel(
            half_kernel,
            [shape(count, 384, width, dtype=BF16) for count in YSPLIT],
            1.0,
            keep,
            *received,
        )
        halves.append((keep, received, sent, [y_swap(part) for part in sent]))

    total, ready, finished = None, None, []
    for i, width in enumerate(CHUNKS):
        keep, received, sent, others = halves[i]
        last = i == len(CHUNKS) - 1
        if ready is not None:
            others = [after(others[0], *ready), *others[1:]]
        (mine,) = local_kernel(
            delta_kernel,
            [shape(3, 384, width, dtype=BF16)],
            width / 300,
            keep,
            *received,
            *others,
        )
        theirs = core_swap(mine)
        if GA_AFTER and not last:
            theirs = after(theirs, *halves[i + 1][2])
        outs = [shape(4, 768, 256)]
        if last:
            outs = [shape(768, 256)] + [shape(768, 256, dtype=BF16)] * 3

        def run_input(theirs):
            return local_kernel(
                functools.partial(input_kernel, columns[i], last, total is not None),
                outs,
                3.0,
                numbers,
                mine,
                theirs,
                *rows[i],
                *(() if total is None else (total,)),
                scalars=1,
                scratch=(pltpu.VMEM((2, 1024, width), BF16), pltpu.VMEM((768, width), BF16)),
            )

        def run_grad(theirs):
            return local_kernel(
                grad_kernel,
                [shape(768, width)] * 2
                + [shape(384, width, dtype=BF16)] * 2
                + [shape(768, width)],
                3.0,
                *turned,
                mine,
                theirs,
                scratch=(pltpu.VMEM((768, width), BF16),),
            )

        if last and INPUT_FIRST:
            partial = run_input(theirs)
            b0, b1, low, high, b3 = run_grad(after(theirs, partial[1]))
        else:
            b0, b1, low, high, b3 = run_grad(theirs)
            partial = run_input(after(theirs, low))
        total = partial[0]
        ahead, behind = local_kernel(
            middle_kernel,
            [shape(768, width, dtype=BF16)] * 2,
            1.0,
            b1,
            b3,
            z_shift(low, 1),
            z_shift(high, -1),
        )
        finished += [b0, z_shift(ahead, 1), z_shift(behind, -1)]
        ready = (*finished[-2:], total)

    blocks = local_kernel(
        column_kernel,
        [shape(192, 256)] * 4,
        1.0,
        numbers,
        partial[0],
        x_shift(partial[1], 1),
        x_shift(partial[2], 2),
        x_shift(partial[3], -1),
        scalars=1,
    )
    moved = [
        _move(
            blocks[2 * j + i],
            lambda z, yl, c, x, yh, i=i, j=j: (z, yh ^ i, c ^ j, x, yl),
        )
        for j in range(2)
        for i in range(2)
    ]
    (input_grad,) = local_kernel(
        place_kernel, [shape(192, 512)], 1.0, numbers, *moved, scalars=1
    )
    gate_grad, up_grad, down_grad = local_kernel(
        finish_kernel, [shape(256, sum(CHUNKS))] * 3, 2.0, *finished
    )
    return (input_grad, gate_grad, up_grad, down_grad)


def solution(mesh):
    return jax.shard_map(
        local,
        mesh=mesh,
        in_specs=(
            P("dp", None),
            P(None, "dp", None),
            P("dp", "tensor"),
            P("dp", "tensor"),
            P("dp", "tensor"),
        ),
        out_specs=(P("dp", "tensor"), P("dp", "tensor"), P("dp", "tensor"), P("dp", "tensor")),
        check_vma=False,
    )
```

```python
import functools

import jax
import jax.numpy as jnp
from jax import lax
from jax.experimental import pallas as pl
from jax.experimental.pallas import tpu as pltpu
from jax.sharding import PartitionSpec as P

FF = 14336
F32 = jnp.float32
BF16 = jnp.bfloat16
CHUNKS = (256, 384, 256)
COSTS = {}
ORDER = {"own1": ["nxt0"], "own2": ["nxt1"], "pre2": ["ahead0", "total0"], "half1": ["other0"], "half2": ["other1"], "grad0": ["sent1"], "grad1": ["sent2"], "delta2": ["ahead1", "total1"], "middle1": ["r10", "r30"], "middle2": ["r11", "r31"], "cut2": ["low0"]}
PARTS = 4
CSPLIT = (1, 1, 1)
YSPLIT = (3,)
INPUT_FIRST = True
VMEM = pl.BlockSpec(memory_space=pltpu.VMEM)
HBM = pl.BlockSpec(memory_space=pltpu.HBM)
SMEM = pl.BlockSpec(memory_space=pltpu.SMEM)
PARAMS = pltpu.CompilerParams(vmem_limit_bytes=10 * 1024 * 1024)


def _split(device):
    dp, tensor = divmod(device, 8)
    return dp // 4, (dp // 2) % 2, dp % 2, tensor // 2, tensor % 2


def _join(z, yl, c, x, yh):
    return ((z % 4) * 4 + yl * 2 + c) * 8 + (x % 4) * 2 + yh


def _move(value, where):
    pairs = [(d, _join(*where(*_split(d)))) for d in range(128)]
    return lax.ppermute(value, ("dp", "tensor"), pairs)


def z_shift(value, by):
    return _move(value, lambda z, yl, c, x, yh: (z + by, yl, c, x, yh))


def x_shift(value, by):
    return _move(value, lambda z, yl, c, x, yh: (z, yl, c, x + by, yh))


def core_swap(value):
    return _move(value, lambda z, yl, c, x, yh: (z, yl, 1 - c, x, yh))


def y_swap(value):
    return _move(value, lambda z, yl, c, x, yh: (z, 1 - yl, c, x, yh))


def far_swap(value):
    return _move(value, lambda z, yl, c, x, yh: (z, 1 - yl, 1 - c, x, 1 - yh))


def after(value, *others):
    return lax.optimization_barrier((value, *others))[0]


def shape(*dims, dtype=F32):
    return jax.ShapeDtypeStruct(dims, dtype)


def local_kernel(kernel, outs, name, *args, scalars=0, scratch=()):
    return pl.pallas_call(
        kernel,
        in_specs=[SMEM] * scalars + [VMEM] * (len(args) - scalars),
        out_specs=[VMEM] * len(outs),
        out_shape=outs,
        scratch_shapes=scratch,
        compiler_params=PARAMS,
        cost_estimate=cost(name),
    )(*args)


def cost(name):
    return pl.CostEstimate(
        flops=int(COSTS.get(name, 1.0) * 1.1e9), bytes_accessed=1000, transcendentals=0
    )


def arrange_kernel(numbers, activations, cotangents, *refs):
    outs, (x, later_x, x_sem, sem) = refs[:4], refs[4:]
    rows = [pl.ds(part * (192 // PARTS), 192 // PARTS) for part in range(PARTS)]

    def copy(part, later):
        if later < 0:
            return pltpu.make_async_copy(
                activations.at[rows[part]], x.at[rows[part]], x_sem.at[part]
            )
        return pltpu.make_async_copy(
            cotangents.at[later, rows[part]],
            later_x.at[later, rows[part]],
            sem.at[part, later],
        )

    for part in range(PARTS):
        for later in range(-1, 4):
            copy(part, later).start()
    for part in range(PARTS):
        for later in range(-1, 4):
            copy(part, later).wait()
        for block in range(16):
            columns = pl.ds(pl.multiple_of(numbers[block] * 256, 256), 256)
            out, k = outs[block // 4], block % 4
            out[0, k, rows[part], :] = x[rows[part], columns]
            total = jnp.zeros((192 // PARTS, 256), F32)
            for later in range(4):
                total = total + numbers[16 + later].astype(F32) * later_x[
                    later, rows[part], columns
                ].astype(F32)
            out[1, k, rows[part], :] = total.astype(BF16)


def arrange(numbers, activations, cotangents):
    return pl.pallas_call(
        arrange_kernel,
        in_specs=[SMEM, HBM, HBM],
        out_specs=[VMEM] * 4,
        out_shape=[shape(2, 4, 192, 256, dtype=BF16)] * 4,
        scratch_shapes=[
            pltpu.VMEM((192, 4096), BF16),
            pltpu.VMEM((4, 192, 4096), BF16),
            pltpu.SemaphoreType.DMA((PARTS,)),
            pltpu.SemaphoreType.DMA((PARTS, 4)),
        ],
        compiler_params=pltpu.CompilerParams(vmem_limit_bytes=16 * 1024 * 1024),
        cost_estimate=cost("arrange"),
    )(numbers, *[pltpu.with_memory_space_constraint(v, pltpu.HBM) for v in (activations, cotangents)])


def spread(kept, far, sibling, sibling_far):
    return (kept, y_swap(far), core_swap(sibling), far_swap(sibling_far))


def turn_kernel(t0, t1, t2, t3, *outs):
    for which, out in enumerate(outs):
        for k in range(4):
            whole = jnp.concatenate([t[which, k] for t in (t0, t1, t2, t3)], axis=0)
            out[k * 256 : (k + 1) * 256, :] = whole.T


def stack_kernel(*refs):
    weights, outs, sem = refs[:3], refs[3:-1], refs[-1]
    copies, first = [], 0
    for i, out in enumerate(outs):
        last = first + out.shape[1]
        for m, weight in enumerate(weights):
            copies.append(
                pltpu.make_async_copy(
                    weight.at[:, pl.ds(first, last - first)],
                    out.at[pl.ds(m * 256, 256)],
                    sem.at[i, m],
                )
            )
        first = last
    for copy in copies:
        copy.start()
    for copy in copies:
        copy.wait()


def stack(*weights):
    outs = [shape(768, width, dtype=BF16) for width in CHUNKS]
    return pl.pallas_call(
        stack_kernel,
        in_specs=[HBM] * 3,
        out_specs=[VMEM] * len(outs),
        out_shape=outs,
        scratch_shapes=[pltpu.SemaphoreType.DMA((len(outs), 3))],
        compiler_params=PARAMS,
        cost_estimate=cost("stack"),
    )(*[pltpu.with_memory_space_constraint(v, pltpu.HBM) for v in weights])


def fill(rows, far, low, high, own, nxt, prev):
    far[0:384] = low[...]
    far[384:768] = high[...]
    for m in range(rows.shape[0]):
        for k, part in enumerate((own, nxt, far, prev)):
            rows[m, k * 256 : (k + 1) * 256] = part[m * 256 : (m + 1) * 256]


def part_of(parts, m):
    for part in parts:
        if m < part.shape[0]:
            return part.at[m]
        m -= part.shape[0]


def pre_kernel(t0, t1, t2, t3, own, nxt, low, high, prev, keep, *refs):
    *sends, left, rows, far = refs
    fill(rows, far, low, high, own, nxt, prev)
    for outs, upper, lower in ((sends, t2, t3), ((keep,), t0, t1)):
        for which in range(2):
            for k in range(4):
                left[0:192, k * 256 : (k + 1) * 256] = upper[which, k]
                left[192:384, k * 256 : (k + 1) * 256] = lower[which, k]
            for m in ((0, 1), (2,))[which]:
                part_of(outs, m)[...] = jnp.dot(
                    left[...], rows[m], preferred_element_type=F32
                )


def half_kernel(keep, *refs):
    received, outs = refs[: len(CSPLIT)], refs[len(CSPLIT) :]
    for m in range(3):
        part_of(outs, m)[...] = (keep[m] + part_of(received, m)[...]).astype(BF16)


def cut_kernel(nxt, prev, low, high):
    low[...] = nxt[0:384]
    high[...] = prev[384:768]


def column_kernel(numbers, own, r1, r2, r3, *outs):
    for j in range(2):
        for i in range(2):
            block = (i + numbers[24]) % 2
            rows = pl.ds(pl.multiple_of(j * 384 + block * 192, 192), 192)
            outs[2 * j + i][...] = (
                own[rows]
                + r1[rows].astype(F32)
                + r2[rows].astype(F32)
                + r3[rows].astype(F32)
            )


def place_kernel(numbers, a0, a1, b0, b1, out):
    for j, (first, second) in enumerate(((a0, a1), (b0, b1))):
        side = (j + numbers[25]) % 2
        out[:, pl.ds(pl.multiple_of(side * 256, 256), 256)] = first[...] + second[...]


def delta_kernel(keep, *refs):
    *refs, out = refs
    received, others = refs[: len(CSPLIT)], refs[len(CSPLIT) :]

    def part(first, swapped):
        @pl.loop(0, 192 // 16)
        def _(i):
            mine = pl.ds(pl.multiple_of(first + i * 16, 16), 16)
            theirs = pl.ds(pl.multiple_of(swapped + i * 16, 16), 16)
            gate, up, grad = (
                (keep[m, mine] + part_of(received, m)[mine])
                + part_of(others, m)[theirs].astype(F32)
                for m in range(3)
            )
            sigmoid = jax.nn.sigmoid(gate)
            silu = gate * sigmoid
            out[0, mine] = (grad * up * sigmoid * (1.0 + gate * (1.0 - sigmoid))).astype(BF16)
            out[1, mine] = (grad * silu).astype(BF16)
            out[2, mine] = (silu * up).astype(BF16)

    part(0, 192)
    part(192, 0)


def grad_kernel(tokens, cotangents, mine, theirs, b0, b1, low, high, b3, right):
    for m in range(3):
        right[0:384] = mine[m]
        right[384:768] = theirs[m]
        left = tokens if m < 2 else cotangents
        for k in (2, 1, 3, 0):
            block = jnp.dot(
                left[k * 256 : (k + 1) * 256, :], right[...], preferred_element_type=F32
            )
            if k != 2:
                (b0, b1, None, b3)[k][m * 256 : (m + 1) * 256] = block
                continue
            block = block.astype(BF16)
            if m == 0:
                low[0:256] = block
            elif m == 1:
                low[256:384] = block[:128]
                high[0:128] = block[128:]
            else:
                high[128:384] = block


def middle_kernel(b1, b3, low, high, ahead, behind):
    ahead[0:384] = (b1[0:384] + low[...].astype(F32)).astype(BF16)
    ahead[384:768] = b1[384:768].astype(BF16)
    behind[0:384] = b3[0:384].astype(BF16)
    behind[384:768] = (b3[384:768] + high[...].astype(F32)).astype(BF16)


def finish_kernel(*refs):
    parts, outs = refs[:-3], refs[-3:]
    for m, out in enumerate(outs):
        rows = slice(m * 256, (m + 1) * 256)
        first = 0
        for i in range(len(parts) // 3):
            b0, r1, r3 = parts[3 * i : 3 * i + 3]
            last = first + b0.shape[1]
            out[:, first:last] = b0[rows] + r1[rows].astype(F32) + r3[rows].astype(F32)
            first = last


def input_kernel(last, has_total, numbers, mine, theirs, own, nxt, low, high, prev, *refs):
    if has_total:
        total, *refs = refs
    *outs, rows, far = refs
    fill(rows, far, low, high, own, nxt, prev)
    over_units = (((1,), (1,)), ((), ()))
    for j in range(4):
        here = pl.ds(pl.multiple_of(numbers[20 + j] * 256, 256), 256)
        for part, delta in enumerate((mine, theirs)):
            tokens = slice(part * 384, (part + 1) * 384)
            block = lax.dot_general(
                delta[0], rows[0, here, :], over_units, preferred_element_type=F32
            ) + lax.dot_general(delta[1], rows[1, here, :], over_units, preferred_element_type=F32)
            if has_total:
                block = block + total[j, tokens]
            if last:
                outs[j][tokens] = block.astype(outs[j].dtype)
            else:
                outs[0][j, tokens] = block


def local(activations, cotangents, gate_weight, up_weight, down_weight):
    dp, tensor = lax.axis_index("dp"), lax.axis_index("tensor")
    z, yl, c = dp // 4, (dp // 2) % 2, dp % 2
    x, yh = tensor // 2, tensor % 2
    first_unit = tensor * gate_weight.shape[1]
    band_index = (
        1
        + (first_unit >= FF // 8).astype(jnp.int32)
        + (first_unit >= FF // 4).astype(jnp.int32)
        + (first_unit >= FF // 2).astype(jnp.int32)
    )
    source = [
        ((z + k) % 4) * 4 + (yl ^ far) * 2 + (c ^ sibling)
        for sibling in range(2)
        for far in range(2)
        for k in range(4)
    ]
    included = [(k + 1 >= band_index).astype(jnp.int32) for k in range(4)]
    order = [(x + j - z) % 4 for j in range(4)]
    numbers = jnp.stack(source + included + order + [(yh + yl) % 2, c]).astype(jnp.int32)

    stacks = stack(gate_weight, up_weight, down_weight)

    def first_step(own):
        return own, z_shift(own, -1), z_shift(own, 1)

    def second_step(own, nxt, prev):
        low, high = local_kernel(
            cut_kernel, [shape(384, own.shape[1], dtype=BF16)] * 2, "cut", nxt, prev
        )
        return own, nxt, z_shift(low, -1), z_shift(high, 1), prev

    pieces = spread(*arrange(numbers, activations, cotangents))
    turned = local_kernel(turn_kernel, [shape(1024, 768, dtype=BF16)] * 2, "turn", *pieces)

    known, rows, halves = {}, [], []

    def hold(stage, value):
        names = ORDER.get(stage, ())
        return after(value, *[known[name] for name in names]) if names else value

    near = [first_step(stacks[0])]

    def forward(i, width):
        own, nxt, prev = near[0]
        known[f"nxt{i}"], known[f"prev{i}"] = nxt, prev
        rows.append(second_step(own, hold(f"cut{i}", nxt), prev))
        if i + 1 < len(CHUNKS):
            near[0] = first_step(hold(f"own{i + 1}", stacks[i + 1]))
        late = pieces[0] if i == 0 else after(pieces[0], *turned)
        keep, *send = local_kernel(
            pre_kernel,
            [shape(3, 384, width)] + [shape(count, 384, width) for count in CSPLIT],
            f"pre{i}",
            hold(f"pre{i}", late),
            *pieces[1:],
            *rows[i],
            scratch=(
                pltpu.VMEM((384, 1024), BF16),
                pltpu.VMEM((3, 1024, width), BF16),
                pltpu.VMEM((768, width), BF16),
            ),
        )
        received = [core_swap(part) for part in send]
        sent = local_kernel(
            half_kernel,
            [shape(count, 384, width, dtype=BF16) for count in YSPLIT],
            f"half{i}",
            hold(f"half{i}", keep),
            *received,
        )
        others = [y_swap(part) for part in sent]
        known[f"sent{i}"], known[f"other{i}"] = sent[0], others[0]
        halves.append((keep, received, others))

    finished, totals = [], [None]

    def backward(i, width):
        total = totals[0]
        keep, received, others = halves[i]
        last = i == len(CHUNKS) - 1
        (mine,) = local_kernel(
            delta_kernel,
            [shape(3, 384, width, dtype=BF16)],
            f"delta{i}",
            hold(f"delta{i}", keep),
            *received,
            *others,
        )
        theirs = core_swap(mine)
        outs = [shape(4, 768, 256)]
        if last:
            outs = [shape(768, 256)] + [shape(768, 256, dtype=BF16)] * 3

        def run_input(theirs):
            return local_kernel(
                functools.partial(input_kernel, last, total is not None),
                outs,
                f"input{i}",
                numbers,
                mine,
                hold(f"input{i}", theirs),
                *rows[i],
                *(() if total is None else (total,)),
                scalars=1,
                scratch=(pltpu.VMEM((2, 1024, width), BF16), pltpu.VMEM((768, width), BF16)),
            )

        def run_grad(theirs):
            return local_kernel(
                grad_kernel,
                [shape(768, width)] * 2
                + [shape(384, width, dtype=BF16)] * 2
                + [shape(768, width)],
                f"grad{i}",
                *turned,
                mine,
                hold(f"grad{i}", theirs),
                scratch=(pltpu.VMEM((768, width), BF16),),
            )

        if last and INPUT_FIRST:
            partial = run_input(theirs)
            b0, b1, low, high, b3 = run_grad(after(theirs, partial[1]))
        else:
            b0, b1, low, high, b3 = run_grad(theirs)
            partial = run_input(after(theirs, low))
        totals[0] = total = partial[0]
        known[f"total{i}"] = total
        ahead, behind = local_kernel(
            middle_kernel,
            [shape(768, width, dtype=BF16)] * 2,
            f"middle{i}",
            hold(f"middle{i}", b1),
            b3,
            z_shift(low, 1),
            z_shift(high, -1),
        )
        finished.extend([b0, z_shift(ahead, 1), z_shift(behind, -1)])
        known[f"ahead{i}"] = ahead
        known[f"r1{i}"], known[f"r3{i}"] = finished[-2:]
        known[f"low{i}"] = low
        return partial

    for i, width in enumerate(CHUNKS):
        forward(i, width)
        if i:
            backward(i - 1, CHUNKS[i - 1])
    partial = backward(len(CHUNKS) - 1, CHUNKS[-1])

    blocks = local_kernel(
        column_kernel,
        [shape(192, 256)] * 4,
        "column",
        numbers,
        partial[0],
        x_shift(partial[1], 1),
        x_shift(partial[2], 2),
        x_shift(partial[3], -1),
        scalars=1,
    )
    moved = [
        _move(
            blocks[2 * j + i],
            lambda z, yl, c, x, yh, i=i, j=j: (z, yh ^ i, c ^ j, x, yl),
        )
        for j in range(2)
        for i in range(2)
    ]
    (input_grad,) = local_kernel(
        place_kernel, [shape(192, 512)], "place", numbers, *moved, scalars=1
    )
    gate_grad, up_grad, down_grad = local_kernel(
        finish_kernel, [shape(256, sum(CHUNKS))] * 3, "finish", *finished
    )
    return (input_grad, gate_grad, up_grad, down_grad)


def solution(mesh):
    return jax.shard_map(
        local,
        mesh=mesh,
        in_specs=(
            P("dp", None),
            P(None, "dp", None),
            P("dp", "tensor"),
            P("dp", "tensor"),
            P("dp", "tensor"),
        ),
        out_specs=(P("dp", "tensor"), P("dp", "tensor"), P("dp", "tensor"), P("dp", "tensor")),
        check_vma=False,
    )
```

```python
import functools

import jax
import jax.numpy as jnp
from jax import lax
from jax.experimental import pallas as pl
from jax.experimental.pallas import tpu as pltpu
from jax.sharding import PartitionSpec as P

FF = 14336
F32 = jnp.float32
BF16 = jnp.bfloat16
CHUNKS = (256, 384, 256)
COSTS = {}
MIX = BF16
ORDER = {"own1": ["nxt0"], "own2": ["nxt1"], "pre2": ["ahead0", "total0"], "half1": ["other0"], "half2": ["other1"], "grad0": ["sent1"], "grad1": ["sent2"], "delta2": ["ahead1", "total1"], "middle1": ["r10", "r30"], "middle2": ["r11", "r31"], "cut2": ["low0"], "cut1": ["turned"], "delta1": ["sent2"]}
PARTS = 4
CSPLIT = (1, 1, 1)
YSPLIT = (3,)
INPUT_FIRST = True
VMEM = pl.BlockSpec(memory_space=pltpu.VMEM)
HBM = pl.BlockSpec(memory_space=pltpu.HBM)
SMEM = pl.BlockSpec(memory_space=pltpu.SMEM)
PARAMS = pltpu.CompilerParams(vmem_limit_bytes=10 * 1024 * 1024)


def _split(device):
    dp, tensor = divmod(device, 8)
    return dp // 4, (dp // 2) % 2, dp % 2, tensor // 2, tensor % 2


def _join(z, yl, c, x, yh):
    return ((z % 4) * 4 + yl * 2 + c) * 8 + (x % 4) * 2 + yh


def _move(value, where):
    pairs = [(d, _join(*where(*_split(d)))) for d in range(128)]
    return lax.ppermute(value, ("dp", "tensor"), pairs)


def z_shift(value, by):
    return _move(value, lambda z, yl, c, x, yh: (z + by, yl, c, x, yh))


def x_shift(value, by):
    return _move(value, lambda z, yl, c, x, yh: (z, yl, c, x + by, yh))


def core_swap(value):
    return _move(value, lambda z, yl, c, x, yh: (z, yl, 1 - c, x, yh))


def y_swap(value):
    return _move(value, lambda z, yl, c, x, yh: (z, 1 - yl, c, x, yh))


def far_swap(value):
    return _move(value, lambda z, yl, c, x, yh: (z, 1 - yl, 1 - c, x, 1 - yh))


def after(value, *others):
    return lax.optimization_barrier((value, *others))[0]


def shape(*dims, dtype=F32):
    return jax.ShapeDtypeStruct(dims, dtype)


def local_kernel(kernel, outs, name, *args, scalars=0, scratch=()):
    return pl.pallas_call(
        kernel,
        in_specs=[SMEM] * scalars + [VMEM] * (len(args) - scalars),
        out_specs=[VMEM] * len(outs),
        out_shape=outs,
        scratch_shapes=scratch,
        compiler_params=PARAMS,
        cost_estimate=cost(name),
    )(*args)


def cost(name):
    return pl.CostEstimate(
        flops=int(COSTS.get(name, 1.0) * 1.1e9), bytes_accessed=1000, transcendentals=0
    )


def arrange_kernel(numbers, activations, cotangents, *refs):
    outs, (x, later_x, x_sem, sem) = refs[:4], refs[4:]
    rows = [pl.ds(part * (192 // PARTS), 192 // PARTS) for part in range(PARTS)]

    def copy(part, later):
        if later < 0:
            return pltpu.make_async_copy(
                activations.at[rows[part]], x.at[rows[part]], x_sem.at[part]
            )
        return pltpu.make_async_copy(
            cotangents.at[later, rows[part]],
            later_x.at[later, rows[part]],
            sem.at[part, later],
        )

    for part in range(PARTS):
        for later in range(-1, 4):
            copy(part, later).start()
    for part in range(PARTS):
        for later in range(-1, 4):
            copy(part, later).wait()
        for block in range(16):
            columns = pl.ds(pl.multiple_of(numbers[block] * 256, 256), 256)
            out, k = outs[block // 4], block % 4
            out[0, k, rows[part], :] = x[rows[part], columns]
            total = jnp.zeros((192 // PARTS, 256), F32)
            for later in range(4):
                total = total + numbers[16 + later].astype(F32) * later_x[
                    later, rows[part], columns
                ].astype(F32)
            out[1, k, rows[part], :] = total.astype(BF16)


def arrange(numbers, activations, cotangents):
    return pl.pallas_call(
        arrange_kernel,
        in_specs=[SMEM, HBM, HBM],
        out_specs=[VMEM] * 4,
        out_shape=[shape(2, 4, 192, 256, dtype=BF16)] * 4,
        scratch_shapes=[
            pltpu.VMEM((192, 4096), BF16),
            pltpu.VMEM((4, 192, 4096), BF16),
            pltpu.SemaphoreType.DMA((PARTS,)),
            pltpu.SemaphoreType.DMA((PARTS, 4)),
        ],
        compiler_params=pltpu.CompilerParams(vmem_limit_bytes=16 * 1024 * 1024),
        cost_estimate=cost("arrange"),
    )(numbers, *[pltpu.with_memory_space_constraint(v, pltpu.HBM) for v in (activations, cotangents)])


def spread(kept, far, sibling, sibling_far):
    return (kept, y_swap(far), core_swap(sibling), far_swap(sibling_far))


def turn_kernel(t0, t1, t2, t3, *outs):
    for which, out in enumerate(outs):
        for k in range(4):
            whole = jnp.concatenate([t[which, k] for t in (t0, t1, t2, t3)], axis=0)
            out[k * 256 : (k + 1) * 256, :] = whole.T


def stack_kernel(*refs):
    weights, outs, sem = refs[:3], refs[3:-1], refs[-1]
    copies, first = [], 0
    for i, out in enumerate(outs):
        last = first + out.shape[1]
        for m, weight in enumerate(weights):
            copies.append(
                pltpu.make_async_copy(
                    weight.at[:, pl.ds(first, last - first)],
                    out.at[pl.ds(m * 256, 256)],
                    sem.at[i, m],
                )
            )
        first = last
    for copy in copies:
        copy.start()
    for copy in copies:
        copy.wait()


def stack(*weights):
    outs = [shape(768, width, dtype=BF16) for width in CHUNKS]
    return pl.pallas_call(
        stack_kernel,
        in_specs=[HBM] * 3,
        out_specs=[VMEM] * len(outs),
        out_shape=outs,
        scratch_shapes=[pltpu.SemaphoreType.DMA((len(outs), 3))],
        compiler_params=PARAMS,
        cost_estimate=cost("stack"),
    )(*[pltpu.with_memory_space_constraint(v, pltpu.HBM) for v in weights])


def fill(rows, far, low, high, own, nxt, prev):
    far[0:384] = low[...]
    far[384:768] = high[...]
    for m in range(rows.shape[0]):
        for k, part in enumerate((own, nxt, far, prev)):
            rows[m, k * 256 : (k + 1) * 256] = part[m * 256 : (m + 1) * 256]


def part_of(parts, m):
    for part in parts:
        if m < part.shape[0]:
            return part.at[m]
        m -= part.shape[0]


def pre_kernel(t0, t1, t2, t3, own, nxt, low, high, prev, keep, *refs):
    *sends, left, rows, far = refs
    fill(rows, far, low, high, own, nxt, prev)
    for outs, upper, lower in ((sends, t2, t3), ((keep,), t0, t1)):
        for which in range(2):
            for k in range(4):
                left[0:192, k * 256 : (k + 1) * 256] = upper[which, k]
                left[192:384, k * 256 : (k + 1) * 256] = lower[which, k]
            for m in ((0, 1), (2,))[which]:
                part_of(outs, m)[...] = jnp.dot(
                    left[...], rows[m], preferred_element_type=F32
                )


def half_kernel(keep, *refs):
    received, outs = refs[: len(CSPLIT)], refs[len(CSPLIT) :]
    for m in range(3):
        part_of(outs, m)[...] = (keep[m] + part_of(received, m)[...]).astype(BF16)


def cut_kernel(nxt, prev, low, high):
    low[...] = nxt[0:384]
    high[...] = prev[384:768]


def column_kernel(numbers, own, r1, r2, r3, *outs):
    for j in range(2):
        for i in range(2):
            block = (i + numbers[24]) % 2
            rows = pl.ds(pl.multiple_of(j * 384 + block * 192, 192), 192)
            total = (
                own[rows]
                + r1[rows].astype(F32)
                + r2[rows].astype(F32)
                + r3[rows].astype(F32)
            )
            outs[2 * j + i][...] = total.astype(MIX)


def place_kernel(numbers, a0, a1, b0, b1, out):
    for j, (first, second) in enumerate(((a0, a1), (b0, b1))):
        side = (j + numbers[25]) % 2
        out[:, pl.ds(pl.multiple_of(side * 256, 256), 256)] = first[...].astype(
            F32
        ) + second[...].astype(F32)


def delta_kernel(keep, *refs):
    *refs, out = refs
    received, others = refs[: len(CSPLIT)], refs[len(CSPLIT) :]

    def part(first, swapped):
        @pl.loop(0, 192 // 16)
        def _(i):
            mine = pl.ds(pl.multiple_of(first + i * 16, 16), 16)
            theirs = pl.ds(pl.multiple_of(swapped + i * 16, 16), 16)
            gate, up, grad = (
                (keep[m, mine] + part_of(received, m)[mine])
                + part_of(others, m)[theirs].astype(F32)
                for m in range(3)
            )
            sigmoid = jax.nn.sigmoid(gate)
            silu = gate * sigmoid
            out[0, mine] = (grad * up * sigmoid * (1.0 + gate * (1.0 - sigmoid))).astype(BF16)
            out[1, mine] = (grad * silu).astype(BF16)
            out[2, mine] = (silu * up).astype(BF16)

    part(0, 192)
    part(192, 0)


def grad_kernel(tokens, cotangents, mine, theirs, b0, b1, low, high, b3, right):
    for m in range(3):
        right[0:384] = mine[m]
        right[384:768] = theirs[m]
        left = tokens if m < 2 else cotangents
        for k in (2, 1, 3, 0):
            block = jnp.dot(
                left[k * 256 : (k + 1) * 256, :], right[...], preferred_element_type=F32
            )
            if k != 2:
                (b0, b1, None, b3)[k][m * 256 : (m + 1) * 256] = block
                continue
            block = block.astype(BF16)
            if m == 0:
                low[0:256] = block
            elif m == 1:
                low[256:384] = block[:128]
                high[0:128] = block[128:]
            else:
                high[128:384] = block


def middle_kernel(b1, b3, low, high, ahead, behind):
    ahead[0:384] = (b1[0:384] + low[...].astype(F32)).astype(BF16)
    ahead[384:768] = b1[384:768].astype(BF16)
    behind[0:384] = b3[0:384].astype(BF16)
    behind[384:768] = (b3[384:768] + high[...].astype(F32)).astype(BF16)


def finish_kernel(first, b0, r1, r3, *refs):
    outs, total, sem = refs[-5:-2], refs[-2], refs[-1]
    copies = []
    for m, out in enumerate(outs):
        rows = slice(m * 256, (m + 1) * 256)
        total[m] = b0[rows] + r1[rows].astype(F32) + r3[rows].astype(F32)
        copies.append(
            pltpu.make_async_copy(
                total.at[m], out.at[:, pl.ds(first, total.shape[2])], sem.at[m]
            )
        )
        copies[-1].start()
    for copy in copies:
        copy.wait()


def finish(first, parts, base):
    width = parts[0].shape[1]
    return pl.pallas_call(
        functools.partial(finish_kernel, first),
        in_specs=[VMEM] * 3 + [HBM] * len(base),
        out_specs=[HBM] * 3,
        out_shape=[shape(256, sum(CHUNKS))] * 3,
        input_output_aliases={3 + m: m for m in range(len(base))},
        scratch_shapes=[pltpu.VMEM((3, 256, width), F32), pltpu.SemaphoreType.DMA((3,))],
        compiler_params=PARAMS,
        cost_estimate=cost("finish"),
    )(*parts, *base)


def input_kernel(last, has_total, numbers, mine, theirs, own, nxt, low, high, prev, *refs):
    if has_total:
        total, *refs = refs
    *outs, rows, far = refs
    fill(rows, far, low, high, own, nxt, prev)
    over_units = (((1,), (1,)), ((), ()))
    for j in range(4):
        here = pl.ds(pl.multiple_of(numbers[20 + j] * 256, 256), 256)
        for part, delta in enumerate((mine, theirs)):
            tokens = slice(part * 384, (part + 1) * 384)
            block = lax.dot_general(
                delta[0], rows[0, here, :], over_units, preferred_element_type=F32
            ) + lax.dot_general(delta[1], rows[1, here, :], over_units, preferred_element_type=F32)
            if has_total:
                block = block + total[j, tokens]
            if last:
                outs[j][tokens] = block.astype(outs[j].dtype)
            else:
                outs[0][j, tokens] = block


def local(activations, cotangents, gate_weight, up_weight, down_weight):
    dp, tensor = lax.axis_index("dp"), lax.axis_index("tensor")
    z, yl, c = dp // 4, (dp // 2) % 2, dp % 2
    x, yh = tensor // 2, tensor % 2
    first_unit = tensor * gate_weight.shape[1]
    band_index = (
        1
        + (first_unit >= FF // 8).astype(jnp.int32)
        + (first_unit >= FF // 4).astype(jnp.int32)
        + (first_unit >= FF // 2).astype(jnp.int32)
    )
    source = [
        ((z + k) % 4) * 4 + (yl ^ far) * 2 + (c ^ sibling)
        for sibling in range(2)
        for far in range(2)
        for k in range(4)
    ]
    included = [(k + 1 >= band_index).astype(jnp.int32) for k in range(4)]
    order = [(x + j - z) % 4 for j in range(4)]
    numbers = jnp.stack(source + included + order + [(yh + yl) % 2, c]).astype(jnp.int32)

    stacks = stack(gate_weight, up_weight, down_weight)

    def first_step(own):
        return own, z_shift(own, -1), z_shift(own, 1)

    def second_step(own, nxt, prev):
        low, high = local_kernel(
            cut_kernel, [shape(384, own.shape[1], dtype=BF16)] * 2, "cut", nxt, prev
        )
        return own, nxt, z_shift(low, -1), z_shift(high, 1), prev

    pieces = spread(*arrange(numbers, activations, cotangents))
    turned = local_kernel(turn_kernel, [shape(1024, 768, dtype=BF16)] * 2, "turn", *pieces)

    known, rows, halves = {f"t{i}": piece for i, piece in enumerate(pieces)}, [], []
    known["turned"] = turned[0]

    def hold(stage, value):
        names = ORDER.get(stage, ())
        return after(value, *[known[name] for name in names]) if names else value

    near = [first_step(stacks[0])]

    def forward(i, width):
        own, nxt, prev = near[0]
        known[f"nxt{i}"], known[f"prev{i}"] = nxt, prev
        rows.append(second_step(own, hold(f"cut{i}", nxt), prev))
        if i + 1 < len(CHUNKS):
            near[0] = first_step(hold(f"own{i + 1}", stacks[i + 1]))
            known[f"nxt{i + 1}"], known[f"prev{i + 1}"] = near[0][1:]
        late = pieces[0] if i != 1 else after(pieces[0], *turned)
        keep, *send = local_kernel(
            pre_kernel,
            [shape(3, 384, width)] + [shape(count, 384, width) for count in CSPLIT],
            f"pre{i}",
            hold(f"pre{i}", late),
            *pieces[1:],
            *rows[i],
            scratch=(
                pltpu.VMEM((384, 1024), BF16),
                pltpu.VMEM((3, 1024, width), BF16),
                pltpu.VMEM((768, width), BF16),
            ),
        )
        received = [core_swap(part) for part in send]
        sent = local_kernel(
            half_kernel,
            [shape(count, 384, width, dtype=BF16) for count in YSPLIT],
            f"half{i}",
            hold(f"half{i}", keep),
            *received,
        )
        others = [y_swap(part) for part in sent]
        known[f"sent{i}"], known[f"other{i}"] = sent[0], others[0]
        halves.append((keep, received, others))

    finished, totals = [], [None]

    def backward(i, width):
        total = totals[0]
        keep, received, others = halves[i]
        last = i == len(CHUNKS) - 1
        (mine,) = local_kernel(
            delta_kernel,
            [shape(3, 384, width, dtype=BF16)],
            f"delta{i}",
            hold(f"delta{i}", keep),
            *received,
            *others,
        )
        theirs = core_swap(mine)
        outs = [shape(4, 768, 256)]
        if last:
            outs = [shape(768, 256)] + [shape(768, 256, dtype=BF16)] * 3

        def run_input(theirs):
            return local_kernel(
                functools.partial(input_kernel, last, total is not None),
                outs,
                f"input{i}",
                numbers,
                mine,
                hold(f"input{i}", theirs),
                *rows[i],
                *(() if total is None else (total,)),
                scalars=1,
                scratch=(pltpu.VMEM((2, 1024, width), BF16), pltpu.VMEM((768, width), BF16)),
            )

        def run_grad(theirs):
            return local_kernel(
                grad_kernel,
                [shape(768, width)] * 2
                + [shape(384, width, dtype=BF16)] * 2
                + [shape(768, width)],
                f"grad{i}",
                *turned,
                mine,
                hold(f"grad{i}", theirs),
                scratch=(pltpu.VMEM((768, width), BF16),),
            )

        if last and INPUT_FIRST:
            partial = run_input(theirs)
            b0, b1, low, high, b3 = run_grad(after(theirs, partial[1]))
        else:
            b0, b1, low, high, b3 = run_grad(theirs)
            partial = run_input(after(theirs, low))
        totals[0] = total = partial[0]
        known[f"total{i}"] = total
        ahead, behind = local_kernel(
            middle_kernel,
            [shape(768, width, dtype=BF16)] * 2,
            f"middle{i}",
            hold(f"middle{i}", b1),
            b3,
            z_shift(low, 1),
            z_shift(high, -1),
        )
        finished.extend([b0, z_shift(ahead, 1), z_shift(behind, -1)])
        known[f"ahead{i}"] = ahead
        known[f"r1{i}"], known[f"r3{i}"] = finished[-2:]
        known[f"low{i}"] = low
        return partial

    for i, width in enumerate(CHUNKS):
        forward(i, width)
        if i:
            backward(i - 1, CHUNKS[i - 1])
    partial = backward(len(CHUNKS) - 1, CHUNKS[-1])

    blocks = local_kernel(
        column_kernel,
        [shape(192, 256, dtype=MIX)] * 4,
        "column",
        numbers,
        partial[0],
        x_shift(partial[1], 1),
        x_shift(partial[2], 2),
        x_shift(partial[3], -1),
        scalars=1,
    )
    moved = [
        _move(
            blocks[2 * j + i],
            lambda z, yl, c, x, yh, i=i, j=j: (z, yh ^ i, c ^ j, x, yl),
        )
        for j in range(2)
        for i in range(2)
    ]
    (input_grad,) = local_kernel(
        place_kernel, [shape(192, 512)], "place", numbers, *moved, scalars=1
    )
    grads = ()
    for i in range(len(CHUNKS)):
        grads = finish(sum(CHUNKS[:i]), finished[3 * i : 3 * i + 3], grads)
    gate_grad, up_grad, down_grad = grads
    return (input_grad, gate_grad, up_grad, down_grad)


def solution(mesh):
    return jax.shard_map(
        local,
        mesh=mesh,
        in_specs=(
            P("dp", None),
            P(None, "dp", None),
            P("dp", "tensor"),
            P("dp", "tensor"),
            P("dp", "tensor"),
        ),
        out_specs=(P("dp", "tensor"), P("dp", "tensor"), P("dp", "tensor"), P("dp", "tensor")),
        check_vma=False,
    )
```
